32 devices in a mesh: parts: 2 (over x), sec: 16 (over z, y, core).
Axes of the slice: x: 2, y: 2, z: 4, core: 2. Of those that a mesh axis runs over, the one named last changes fastest.
Arguments:
- left_env: float32 [128, 13, 128, 128], P(('parts', 'sec')), parts along dimension 0, as said below
- right_env: float32 [128, 13, 128, 128], P(('parts', 'sec')), parts along dimension 0, as said below
- hop_ops: float32 [128, 4, 128, 128], P(('parts', 'sec')), parts along dimension 0, may hold values from -0.5 to 0.5
- start: float32 [128, 128, 128], P(('parts', 'sec')), parts along dimension 0, may hold values from -6 to 6
- left_dims: int32 [128], P(('parts', 'sec')), parts along dimension 0, may hold values from 32 to 128, as said below
- right_dims: int32 [128], P(('parts', 'sec')), parts along dimension 0, may hold values from 32 to 128, as said below
Outputs:
- ritz: float32 [128, 128, 128], P(('parts', 'sec')), parts along dimension 0
- energy: float32 [2], P('parts'), parts along dimension 0
The draws below stay inside these ranges and needn't reach their ends.
There are 2 independent parts, one for each index of `parts`. The reference program is written for one: setup_inputs(seed, part) draws one part's arguments, and reference() takes and returns one part's arrays. A program takes and returns all parts, laid end to end along the dimension named above; each array names one. Nothing has to cross between parts.
Inputs may be any that keep to these rules, and one draw needn't show every extreme that they name: `left_dims`: live rows of a sector; some sector has all 128. `right_dims`: live columns of a sector; some sector has all 128. `left_env`: each block is symmetric. `right_env`: each block is symmetric.
All inputs are finite; a program needn't handle non-finite values.
Results may differ from the reference program's by a relative error of at most 0.0001.
Values sent between devices are 32-bit elements; how exact they have to be, the bound alone decides.
A program may use at most 64 MiB of HBM per device.

```python
import math
import jax
import jax.numpy as jnp
from jax import lax

B = 128
W = 13
ITERS = 4
SECTORS = 64


def symmetric_blocks(key):
    normals = jax.random.normal(key, (SECTORS, W, B, B), jnp.float32)
    blocks = (normals + jnp.swapaxes(normals, -1, -2)) * (0.5 / math.sqrt(B))
    return blocks


def draw_left_env(key, part):
    key = jax.random.fold_in(key, 11)
    return symmetric_blocks(key)


def draw_right_env(key, part):
    key = jax.random.fold_in(key, 12)
    return symmetric_blocks(key)


def live_sizes(key):
    sizes = jax.random.randint(key, (SECTORS,), B // 4, B + 1, jnp.int32)
    chosen = jax.random.randint(jax.random.fold_in(key, 1), (), 0, SECTORS, jnp.int32)
    return jnp.where(jnp.arange(SECTORS, dtype=jnp.int32) == chosen, B, sizes).astype(jnp.int32)


def draw_left_dims(key, part):
    key = jax.random.fold_in(key, 21)
    return live_sizes(key)


def draw_right_dims(key, part):
    key = jax.random.fold_in(key, 22)
    return live_sizes(key)


def block_levels(stream_key, dims, cuts, smallest, largest):
    factor_of = 1.0
    for dim, blocks in cuts:
        draws = jax.random.uniform(jax.random.fold_in(jax.random.fold_in(stream_key, 6), dim), (blocks,), jnp.float32, smallest / len(cuts), largest / len(cuts))
        factor_of = factor_of * jnp.repeat(jnp.exp(draws), dims[dim] // blocks).reshape((-1,) + (1,) * (len(dims) - 1 - dim))
    return factor_of


def bell_draw(key, dims, spread, most, pieces=(), kind=jnp.bfloat16):
    gain = block_levels(key, dims, pieces, -0.22, 0.18) if pieces else 1.0
    array = jax.random.normal(key, dims, jnp.float32) * spread * gain
    return jnp.minimum(jnp.maximum(array, -most), most).astype(kind)


def setup_inputs(seed: int = 0, part: int = 0) -> dict:
    streams_of = jax.random.split(jax.random.key(seed), 7)
    part_splits = jax.random.split(jax.random.fold_in(streams_of[6], part), 7)
    left_env = draw_left_env(jax.random.fold_in(jax.random.fold_in(streams_of[6], part), 71), part)
    right_env = draw_right_env(jax.random.fold_in(jax.random.fold_in(streams_of[6], part), 71), part)
    hop_ops = bell_draw(part_splits[2], (SECTORS, 4, B, B), B ** -0.5, 0.5, ((0, 16),), jnp.float32)
    start = bell_draw(part_splits[3], (SECTORS, B, B), 1.0, 6.0, ((0, 16),), jnp.float32)
    left_dims = draw_left_dims(jax.random.fold_in(jax.random.fold_in(streams_of[6], part), 71), part)
    right_dims = draw_right_dims(jax.random.fold_in(jax.random.fold_in(streams_of[6], part), 71), part)
    return {"left_env": left_env, "right_env": right_env, "hop_ops": hop_ops, "start": start, "left_dims": left_dims, "right_dims": right_dims}


highest = lax.Precision.HIGHEST
epsilon = 1e-12

def diagonal_terms(left_env, right_env, blocks):
    partial_left = jnp.einsum('swab,sbc->swac', left_env, blocks, precision=highest)
    return jnp.einsum('swac,swcd->sad', partial_left, right_env, precision=highest)

def forward_term(hop_ops, blocks, offset):
    first = 2 * offset - 2
    partial_left = jnp.einsum('sab,sbc->sac', hop_ops[:, first], blocks, precision=highest)
    return jnp.einsum('sac,scd->sad', partial_left, hop_ops[:, first + 1], precision=highest)

def backward_term(hop_ops, blocks, offset):
    first = 2 * offset - 2
    partial_left = jnp.einsum('sba,sbc->sac', hop_ops[:, first], blocks, precision=highest)
    return jnp.einsum('sac,sdc->sad', partial_left, hop_ops[:, first + 1], precision=highest)

def apply_hamiltonian(left_env, right_env, hop_ops, live_mask, blocks):
    total = diagonal_terms(left_env, right_env, blocks)
    count = blocks.shape[0]
    padded = jnp.pad(blocks, ((2, 2), (0, 0), (0, 0)))
    ops_padded = jnp.pad(hop_ops, ((2, 0), (0, 0), (0, 0), (0, 0)))
    for offset in (1, 2):
        total = total + forward_term(hop_ops, padded[2 + offset:2 + offset + count], offset)
        total = total + backward_term(ops_padded[2 - offset:2 - offset + count], padded[2 - offset:2 - offset + count], offset)
    return live_mask * total

def reference(left_env, right_env, hop_ops, start, left_dims, right_dims):
    block_size = start.shape[1]
    positions = jnp.arange(block_size, dtype=jnp.int32)
    row_live = positions[None, :] < left_dims[:, None]
    col_live = positions[None, :] < right_dims[:, None]
    live_mask = (row_live[:, :, None] & col_live[:, None, :]).astype(jnp.float32)
    masked = live_mask * start
    current = masked / jnp.sqrt(jnp.sum(masked * masked))
    image = apply_hamiltonian(left_env, right_env, hop_ops, live_mask, current)
    lowest = jnp.float32(0.0)
    for iteration in range(ITERS):
        rayleigh = jnp.sum(current * image)
        residual = image - rayleigh * current
        res_norm = jnp.sqrt(jnp.sum(residual * residual) + epsilon)
        direction = residual / res_norm
        bent = apply_hamiltonian(left_env, right_env, hop_ops, live_mask, direction)
        curvature = jnp.sum(direction * bent)
        lowest = (rayleigh + curvature) / 2 - jnp.sqrt(((rayleigh - curvature) / 2) ** 2 + res_norm * res_norm)
        slope = lowest - rayleigh
        length = jnp.sqrt(res_norm * res_norm + slope * slope)
        current = (res_norm * current + slope * direction) / length
        image = (res_norm * image + slope * bent) / length
    total_entries = start.shape[0] * block_size * block_size
    ritz = current * jnp.sqrt(jnp.float32(total_entries))
    return (ritz, jnp.reshape(lowest, (1,)).astype(jnp.float32))
```

```python
import functools
import math

import jax
import jax.numpy as jnp
from jax import lax
from jax.experimental import pallas as pl
from jax.experimental.pallas import tpu as pltpu
from jax.sharding import PartitionSpec as P

ITERS = 4
EPSILON = 1e-12
MESH = pl.DeviceIdType.MESH
f32 = jnp.float32
bf16 = jnp.bfloat16


def halves(x):
    hi = x.astype(bf16)
    return hi, (x - hi.astype(f32)).astype(bf16)


def fold(x):
    return jnp.sum(x, axis=0, keepdims=True)


def kernel(
    n, count, terms,
    left_env, right_env, hop_ops, start, left_dims, right_dims,
    ritz, energy,
    left_in, right_in, hop_in, rim, ops_left, ops_right, ops_halo, middle,
    cur, img, out, halo_in, halo_cur, halo_img, part, sums,
    load_sem, rim_send, rim_recv, halo_send, halo_recv, sum_send, sum_recv,
):
    size = start.shape[1]
    me = lax.axis_index("sec")
    has_left, has_right = me > 0, me < n - 1
    left, right = lax.max(me - 1, 0), lax.min(me + 1, n - 1)
    steps = ITERS + 1

    loads = [pltpu.make_async_copy(start, img, load_sem.at[0]),
             pltpu.make_async_copy(hop_ops, hop_in, load_sem.at[1])]
    for s in range(count):
        loads.append(pltpu.make_async_copy(left_env.at[s], left_in.at[s], load_sem.at[2 + 2 * s]))
        loads.append(pltpu.make_async_copy(right_env.at[s], right_in.at[s], load_sem.at[3 + 2 * s]))
    for load in loads:
        load.start()

    barrier = pltpu.get_barrier_semaphore()

    def greet(j, carry):
        pl.semaphore_signal(barrier, inc=1, device_id={"sec": lax.rem(me + j, n)}, device_id_type=MESH)
        return carry

    lax.fori_loop(1, n, greet, 0)

    rows = lax.broadcasted_iota(jnp.int32, (size, size), 0)
    cols = lax.broadcasted_iota(jnp.int32, (size, size), 1)

    def masked(s, x):
        return jnp.where((rows < left_dims[s]) & (cols < right_dims[s]), x, 0.0)

    zero = jnp.zeros((size, size), f32)
    halo_cur[...] = jnp.zeros_like(halo_cur)
    cur[...] = jnp.zeros_like(cur)

    @pl.when(jnp.logical_not(has_left))
    def _():
        rim[...] = jnp.zeros_like(rim)
        for p in range(steps):
            halo_in[p, 0:2] = jnp.zeros((2, size, size), f32)

    @pl.when(jnp.logical_not(has_right))
    def _():
        for p in range(steps):
            halo_in[p, 2:4] = jnp.zeros((2, size, size), f32)

    scale = 1.0 / (6.0 * math.sqrt(count * n * size * size))
    loads[0].wait()
    for s in range(count):
        img[s] = masked(s, img[s]) * scale

    pl.semaphore_wait(barrier, n - 1)

    def halo_copy(src, p, s, slot):
        device = right if slot < 2 else left
        return pltpu.make_async_remote_copy(
            src_ref=src.at[s], dst_ref=halo_in.at[p, slot],
            send_sem=halo_send.at[p, slot], recv_sem=halo_recv.at[p, slot],
            device_id={"sec": device}, device_id_type=MESH)

    targets = {}
    for i in range(2):
        targets.setdefault(count - 2 + i, []).append(i)
        targets.setdefault(i, []).append(2 + i)

    def halo_start(src, p, s, more=True):
        for slot in targets.get(s, ()):
            @pl.when((has_right if slot < 2 else has_left) & more)
            def _():
                halo_copy(src, p, s, slot).start()

    def halo_wait_send(src, p):
        for s in targets:
            for slot in targets[s]:
                @pl.when(has_right if slot < 2 else has_left)
                def _():
                    halo_copy(src, p, s, slot).wait_send()

    def halo_wait_recv(p):
        for slot in range(4):
            @pl.when(has_left if slot < 2 else has_right)
            def _():
                halo_copy(img, p, 0, slot).wait_recv()

    for s in range(count):
        halo_start(img, 0, s)
    rim_copy = pltpu.make_async_remote_copy(
        src_ref=hop_ops.at[count - 2:count], dst_ref=rim,
        send_sem=rim_send, recv_sem=rim_recv, device_id={"sec": right}, device_id_type=MESH)

    @pl.when(has_right)
    def _():
        rim_copy.start()

    def sum_start(which, p, partial):
        sums[which, p, me] = partial
        part[which] = partial

        def send(j, carry):
            pltpu.make_async_remote_copy(
                src_ref=part.at[which], dst_ref=sums.at[which, p, me],
                send_sem=sum_send.at[which, p], recv_sem=sum_recv.at[which, p],
                device_id={"sec": lax.rem(me + j, n)}, device_id_type=MESH).start()
            return carry

        lax.fori_loop(1, n, send, 0)

    def sum_wait(which, p):
        whole = sums.at[which, p, 0:n - 1]
        pltpu.make_async_copy(whole, whole, sum_recv.at[which, p]).wait()
        pltpu.make_async_copy(whole, whole, sum_send.at[which, p]).wait()
        lanes = jnp.sum(sums[which, p], axis=0)
        return jnp.sum(lanes, axis=1, keepdims=True)

    def put(ref, index, row, x):
        hi, lo = halves(x)
        ref[index, row * size:(row + 1) * size, 0:size] = hi
        ref[index, row * size:(row + 1) * size, size:2 * size] = lo

    hop_rows = [[] for _ in range(count)]
    halo_rows = [[] for _ in range(4)]
    for k in (1, 2):
        for s in range(count):
            t = s + k
            entry = (s, terms + k - 1, s, k, False)
            (hop_rows[t] if t < count else halo_rows[2 + t - count]).append(entry)
            t = s - k
            entry = (s, terms + k + 1, t, k, True)
            (hop_rows[t] if t >= 0 else halo_rows[2 + t]).append(entry)

    def hop(owner, index):
        return hop_in[owner, index] if owner >= 0 else rim[2 + owner, index]

    loads[1].wait()
    for s in range(count):
        loads[2 + 2 * s].wait()
        for w in range(terms):
            put(ops_left, s, w, left_in[s, w])
        for i, (_, _, owner, k, flip) in enumerate(hop_rows[s]):
            block = hop(owner, 2 * k - 2)
            put(ops_left, s, terms + i, block.T if flip else block)
        loads[3 + 2 * s].wait()
        for w in range(terms):
            put(ops_right, s, w, right_in[s, w])
        for k in (1, 2):
            put(ops_right, s, terms + k - 1, hop(s, 2 * k - 1))
            if s - k >= 0:
                put(ops_right, s, terms + k + 1, hop(s - k, 2 * k - 1).T)

    @pl.when(has_left)
    def _():
        rim_copy.wait_recv()

    @pl.when(has_right)
    def _():
        rim_copy.wait_send()

    for slot in range(4):
        for i, (_, _, owner, k, flip) in enumerate(halo_rows[slot]):
            block = hop(owner, 2 * k - 2)
            put(ops_halo, slot, i, block.T if flip else block)
    for s in range(count):
        for k in (1, 2):
            if s - k < 0:
                put(ops_right, s, terms + k + 1, hop(s - k, 2 * k - 1).T)

    halo_wait_recv(0)
    halo_wait_send(img, 0)
    halo_img[...] = halo_in[0]

    def first_stage(ops, index, x, targets_of):
        hi, lo = halves(x)
        line = jnp.concatenate([hi, lo], axis=1)
        both = jnp.concatenate([line, line], axis=0)
        chunk = 4
        for base in range(0, len(targets_of), chunk):
            some = targets_of[base:base + chunk]
            product = jnp.dot(ops[index, base * size:(base + len(some)) * size, :], both,
                              preferred_element_type=f32)
            for i, (s, column) in enumerate(some):
                y = product[i * size:(i + 1) * size]
                hi, lo = halves(y[:, :size] + y[:, size:])
                middle[s, 0:size, column * size:(column + 1) * size] = hi
                middle[s, size:2 * size, column * size:(column + 1) * size] = lo

    order = []
    for s in range((count + 1) // 2):
        order += [s] if s == count - 1 - s else [s, count - 1 - s]

    def step(p, carry):
        partial = jnp.zeros((size, size), f32)
        for s in range(count):
            partial += cur[s] * img[s]
        sum_start(0, p, jnp.concatenate([fold(partial)] * 2, axis=0))

        for t in range(count):
            first_stage(ops_left, t, img[t],
                        [(t, w) for w in range(terms)] + [(e[0], e[1]) for e in hop_rows[t]])
        for slot in range(4):
            first_stage(ops_halo, slot, halo_img[slot], [(e[0], e[1]) for e in halo_rows[slot]])
        for s in order:
            product = jnp.dot(middle[s], ops_right[s], preferred_element_type=f32)
            product = product[:size] + product[size:]
            out[s] = masked(s, product[:, :size] + product[:, size:])
            halo_start(out, p + 1, s, p < ITERS)

        rayleigh = sum_wait(0, p)[0:1]
        square = jnp.zeros((size, size), f32)
        bend = jnp.zeros((size, size), f32)
        for s in range(count):
            residual = img[s] - rayleigh * cur[s]
            square += residual * residual
            bend += residual * (out[s] - rayleigh * img[s])
        sum_start(1, p, jnp.concatenate([fold(square), fold(bend)], axis=0))
        both = sum_wait(1, p)
        first = p == 0
        res_sq = both[0:1] + EPSILON
        res_norm = jnp.sqrt(res_sq)
        curvature = both[1:2] / res_sq
        lowest = (rayleigh + curvature) / 2 - jnp.sqrt(((rayleigh - curvature) / 2) ** 2 + res_norm * res_norm)
        slope = lowest - rayleigh
        length = jnp.sqrt(res_norm * res_norm + slope * slope)
        keep = jnp.where(first, 0.0, res_norm / length)
        move = jnp.where(first, lax.rsqrt(both[0:1]), slope / length / res_norm)
        energy[...] = lowest

        for s in range(count):
            cur[s] = keep * cur[s] + move * (img[s] - rayleigh * cur[s])

        @pl.when(p < ITERS)
        def _():
            for s in range(count):
                img[s] = keep * img[s] + move * (out[s] - rayleigh * img[s])
            halo_wait_recv(p + 1)
            halo_wait_send(out, p + 1)
            for slot in range(4):
                halo_cur[slot], halo_img[slot] = (
                    keep * halo_cur[slot] + move * (halo_img[slot] - rayleigh * halo_cur[slot]),
                    keep * halo_img[slot] + move * (halo_in[p + 1, slot] - rayleigh * halo_img[slot]))

        return carry

    lax.fori_loop(0, steps, step, 0)
    ritz[...] = cur[...]


def on_device(left_env, right_env, hop_ops, start, left_dims, right_dims):
    count, terms, size = left_env.shape[0], left_env.shape[1], left_env.shape[2]
    n = lax.axis_size("sec")
    blocks = terms + 4
    steps = ITERS + 1
    dma = pltpu.SemaphoreType.DMA
    anywhere = pl.BlockSpec(memory_space=pl.ANY)
    scalars = pl.BlockSpec(memory_space=pltpu.SMEM)
    inside = pl.BlockSpec(memory_space=pltpu.VMEM)
    ritz, energy = pl.pallas_call(
        functools.partial(kernel, n, count, terms),
        out_shape=(jax.ShapeDtypeStruct((count, size, size), f32), jax.ShapeDtypeStruct((1, 1), f32)),
        in_specs=[anywhere] * 4 + [scalars] * 2,
        out_specs=(inside, inside),
        scratch_shapes=[
            pltpu.VMEM((count, terms, size, size), f32),
            pltpu.VMEM((count, terms, size, size), f32),
            pltpu.VMEM((count, 4, size, size), f32),
            pltpu.VMEM((2, 4, size, size), f32),
            pltpu.VMEM((count, blocks * size, 2 * size), bf16),
            pltpu.VMEM((count, blocks * size, 2 * size), bf16),
            pltpu.VMEM((4, 2 * size, 2 * size), bf16),
            pltpu.VMEM((count, 2 * size, blocks * size), bf16),
            pltpu.VMEM((count, size, size), f32),
            pltpu.VMEM((count, size, size), f32),
            pltpu.VMEM((count, size, size), f32),
            pltpu.VMEM((steps, 4, size, size), f32),
            pltpu.VMEM((4, size, size), f32),
            pltpu.VMEM((4, size, size), f32),
            pltpu.VMEM((2, 2, size), f32),
            pltpu.VMEM((2, steps, n, 2, size), f32),
            dma((2 + 2 * count,)),
            dma, dma,
            dma((steps, 4)), dma((steps, 4)),
            dma((2, steps)), dma((2, steps)),
        ],
        compiler_params=pltpu.CompilerParams(
            collective_id=0, has_side_effects=True, vmem_limit_bytes=48 * 1024 * 1024),
    )(left_env, right_env, hop_ops, start, left_dims, right_dims)
    total_entries = count * n * size * size
    return ritz * jnp.sqrt(jnp.float32(total_entries)), jnp.reshape(energy, (1,))


def solution(mesh):
    in_specs = (
        P(("parts", "sec"), None, None, None),
        P(("parts", "sec"), None, None, None),
        P(("parts", "sec"), None, None, None),
        P(("parts", "sec"), None, None),
        P(("parts", "sec")),
        P(("parts", "sec")),
    )
    out_specs = (P(("parts", "sec"), None, None), P("parts"))
    return jax.shard_map(
        on_device, mesh=mesh, in_specs=in_specs, out_specs=out_specs, check_vma=False
    )
```

```python
import functools
import math

import jax
import jax.numpy as jnp
from jax import lax
from jax.experimental import pallas as pl
from jax.experimental.pallas import tpu as pltpu
from jax.sharding import PartitionSpec as P

ITERS = 4
EPSILON = 1e-12
MESH = pl.DeviceIdType.MESH
f32 = jnp.float32
bf16 = jnp.bfloat16


def halves(x):
    hi = x.astype(bf16)
    return hi, (x - hi.astype(f32)).astype(bf16)


def kernel(
    n, count, terms,
    left_env, right_env, hop_ops, start, left_dims, right_dims,
    ritz, energy,
    left_in, right_in, hop_in, rim, ops_left, ops_right, ops_halo, middle,
    cur, img, top, own, out, halo_in, halo_top, sums, tops, coef,
    load_sem, rim_send, rim_recv, halo_send, halo_recv, sum_send, sum_recv,
):
    size = start.shape[1]
    me = lax.axis_index("sec")
    has_left, has_right = me > 0, me < n - 1
    left, right = lax.max(me - 1, 0), lax.min(me + 1, n - 1)
    steps = ITERS + 1
    inner = max(d for d in range(1, n + 1) if n % d == 0 and d * d <= n)
    outer = n // inner
    place, group = lax.rem(me, inner), lax.div(me, inner)

    def near(j):
        return group * inner + lax.rem(place + j, inner)

    def far(j):
        return lax.rem(group + j, outer) * inner + place

    loads = [pltpu.make_async_copy(start, top, load_sem.at[0]),
             pltpu.make_async_copy(hop_ops, hop_in, load_sem.at[1])]
    for s in range(count):
        loads.append(pltpu.make_async_copy(left_env.at[s], left_in.at[s], load_sem.at[2 + 2 * s]))
        loads.append(pltpu.make_async_copy(right_env.at[s], right_in.at[s], load_sem.at[3 + 2 * s]))
    for load in loads:
        load.start()

    barrier = pltpu.get_barrier_semaphore()
    left_apart = (place == 0) & has_left
    right_apart = (place == inner - 1) & has_right

    def greet(device):
        pl.semaphore_signal(barrier, inc=1, device_id={"sec": device}, device_id_type=MESH)

    for j in range(1, inner):
        greet(near(j))
    for j in range(1, outer):
        greet(far(j))

    @pl.when(left_apart)
    def _():
        greet(left)

    @pl.when(right_apart)
    def _():
        greet(right)

    rows = lax.broadcasted_iota(jnp.int32, (size, size), 0)
    cols = lax.broadcasted_iota(jnp.int32, (size, size), 1)
    lane = lax.broadcasted_iota(jnp.int32, (1, size), 1)

    def masked(s, x):
        return jnp.where((rows < left_dims[s]) & (cols < right_dims[s]), x, 0.0)

    halo_top[...] = jnp.zeros_like(halo_top)
    cur[...] = jnp.zeros_like(cur)
    img[...] = jnp.zeros_like(img)

    @pl.when(jnp.logical_not(has_left))
    def _():
        rim[...] = jnp.zeros_like(rim)
        for p in range(steps):
            halo_in[p, 0:2] = jnp.zeros((2, size, size), f32)

    @pl.when(jnp.logical_not(has_right))
    def _():
        for p in range(steps):
            halo_in[p, 2:4] = jnp.zeros((2, size, size), f32)

    scale = 1.0 / (6.0 * math.sqrt(count * n * size * size))
    loads[0].wait()
    for s in range(count):
        top[s] = masked(s, top[s]) * scale

    pl.semaphore_wait(
        barrier, inner + outer - 2 + left_apart.astype(jnp.int32) + right_apart.astype(jnp.int32))

    def halo_copy(src, p, s, slot):
        device = right if slot < 2 else left
        return pltpu.make_async_remote_copy(
            src_ref=src.at[s], dst_ref=halo_in.at[p, slot],
            send_sem=halo_send.at[p, slot], recv_sem=halo_recv.at[p, slot],
            device_id={"sec": device}, device_id_type=MESH)

    targets = {}
    for i in range(2):
        targets.setdefault(count - 2 + i, []).append(i)
        targets.setdefault(i, []).append(2 + i)

    def halo_start(src, p, s, more=True):
        for slot in targets.get(s, ()):
            @pl.when((has_right if slot < 2 else has_left) & more)
            def _():
                halo_copy(src, p, s, slot).start()

    def halo_wait(p):
        for s in targets:
            for slot in targets[s]:
                @pl.when(has_right if slot < 2 else has_left)
                def _():
                    halo_copy(out, p, s, slot).wait_send()

                @pl.when(has_left if slot < 2 else has_right)
                def _():
                    halo_copy(out, p, s, slot).wait_recv()

    for s in range(count):
        halo_start(top, 0, s)
    rim_copies = [
        pltpu.make_async_remote_copy(
            src_ref=src, dst_ref=dst, send_sem=rim_send.at[i], recv_sem=rim_recv.at[i],
            device_id={"sec": right}, device_id_type=MESH)
        for i, (src, dst) in enumerate((
            (hop_ops.at[count - 1], rim.at[1]),
            (hop_ops.at[count - 2, 2:4], rim.at[0, 2:4])))]

    @pl.when(has_right)
    def _():
        for copy in rim_copies:
            copy.start()

    def sum_send_all(buffer, which, p, mine, partners):
        for j, device in enumerate(partners):
            pltpu.make_async_remote_copy(
                src_ref=buffer.at[p, mine], dst_ref=buffer.at[p, mine],
                send_sem=sum_send.at[which, p], recv_sem=sum_recv.at[which, p],
                device_id={"sec": device}, device_id_type=MESH).start()

    def sum_wait_all(buffer, which, p, peers):
        if peers == 1:
            return
        whole = buffer.at[p, 0:peers - 1]
        pltpu.make_async_copy(whole, whole, sum_recv.at[which, p]).wait()
        pltpu.make_async_copy(whole, whole, sum_send.at[which, p]).wait()

    def sum_start(p, values):
        line = jnp.zeros((1, size), f32)
        for i, value in enumerate(values):
            line = jnp.where(lane == i, jnp.sum(value, axis=(0, 1), keepdims=True), line)
        sums[p, place] = line
        sum_send_all(sums, 0, p, place, [near(j) for j in range(1, inner)])

    def sum_middle(p):
        sum_wait_all(sums, 0, p, inner)
        tops[p, group] = jnp.sum(sums[p], axis=0)
        sum_send_all(tops, 1, p, group, [far(j) for j in range(1, outer)])

    def sum_end(p):
        sum_wait_all(tops, 1, p, outer)
        line = jnp.sum(tops[p], axis=0)
        return [jnp.broadcast_to(jnp.sum(jnp.where(lane == i, line, 0.0), axis=1, keepdims=True), (1, size))
                for i in range(4)]

    def put(ref, index, row, x):
        hi, lo = halves(x)
        ref[index, row * size:(row + 1) * size, 0:size] = hi
        ref[index, row * size:(row + 1) * size, size:2 * size] = lo

    hop_rows = [[] for _ in range(count)]
    halo_rows = [[] for _ in range(4)]
    seconds = [[] for _ in range(count)]
    own_columns = []
    for s in range(count):
        column = terms
        for inside in (True, False):
            for k in (1, 2):
                for t, owner, flip in ((s + k, s, False), (s - k, s - k, True)):
                    if (0 <= t < count) != inside:
                        continue
                    entry = (s, column, owner, k, flip)
                    if inside:
                        hop_rows[t].append(entry)
                    else:
                        halo_rows[2 + t if t < 0 else 2 + t - count].append(entry)
                    seconds[s].append(entry)
                    column += 1
            if inside:
                own_columns.append(column)

    def hop(owner, index, flip):
        block = hop_in[owner, index] if owner >= 0 else rim[2 + owner, index]
        return block.T if flip else block

    loads[1].wait()
    for s in range(count):
        loads[2 + 2 * s].wait()
        for w in range(terms):
            put(ops_left, s, w, left_in[s, w])
        for i, (_, _, owner, k, flip) in enumerate(hop_rows[s]):
            put(ops_left, s, terms + i, hop(owner, 2 * k - 2, flip))
    for s in range(count):
        loads[3 + 2 * s].wait()
        for w in range(terms):
            put(ops_right, s, w, right_in[s, w])
        for _, column, owner, k, flip in seconds[s]:
            if owner >= 0:
                put(ops_right, s, column, hop(owner, 2 * k - 1, flip))
    for slot in range(4):
        for i, (_, _, owner, k, flip) in enumerate(halo_rows[slot]):
            if owner >= 0:
                put(ops_halo, slot, i, hop(owner, 2 * k - 2, flip))

    def rim_end():
        @pl.when(has_left)
        def _():
            for copy in rim_copies:
                copy.wait_recv()

        @pl.when(has_right)
        def _():
            for copy in rim_copies:
                copy.wait_send()

        for slot in range(4):
            for i, (_, _, owner, k, flip) in enumerate(halo_rows[slot]):
                if owner < 0:
                    put(ops_halo, slot, i, hop(owner, 2 * k - 2, flip))
        for s in range(count):
            for _, column, owner, k, flip in seconds[s]:
                if owner < 0:
                    put(ops_right, s, column, hop(owner, 2 * k - 1, flip))

    def first_stage(ops, index, x, targets_of):
        hi, lo = halves(x)
        line = jnp.concatenate([hi, lo], axis=1)
        both = jnp.concatenate([line, line], axis=0)
        chunk = 4
        for base in range(0, len(targets_of), chunk):
            some = targets_of[base:base + chunk]
            product = jnp.dot(ops[index, base * size:(base + len(some)) * size, :], both,
                              preferred_element_type=f32)
            for i, (s, column) in enumerate(some):
                y = product[i * size:(i + 1) * size]
                hi, lo = halves(y[:, :size] + y[:, size:])
                middle[s, 0:size, column * size:(column + 1) * size] = hi
                middle[s, size:2 * size, column * size:(column + 1) * size] = lo

    def second_stage(s, begin, end):
        product = jnp.dot(middle[s, :, begin * size:end * size], ops_right[s, begin * size:end * size, :],
                          preferred_element_type=f32)
        product = product[:size] + product[size:]
        return product[:, :size] + product[:, size:]

    order = []
    for s in range((count + 1) // 2):
        order += [s] if s == count - 1 - s else [s, count - 1 - s]

    def sums_of(rayleigh):
        values = [jnp.zeros((size, size), f32) for _ in range(4)]
        for s in range(count):
            residual = img[s] - rayleigh * cur[s]
            bent = top[s] - rayleigh * img[s]
            values[0] += residual * residual
            values[1] += residual * bent
            values[2] += cur[s] * bent
            values[3] += residual * img[s]
        return values

    def solve(first, rayleigh, values):
        res_sum, res_bent, cur_bent, res_img = values
        res_sq = res_sum + EPSILON
        res_norm = jnp.sqrt(res_sq)
        curvature = res_bent / res_sq
        lowest = (rayleigh + curvature) / 2 - jnp.sqrt(((rayleigh - curvature) / 2) ** 2 + res_norm * res_norm)
        slope = lowest - rayleigh
        length = jnp.sqrt(res_norm * res_norm + slope * slope)
        keep = jnp.where(first, 0.0, res_norm / length)
        move = jnp.where(first, lax.rsqrt(res_sum), slope / length / res_norm)
        following = keep * keep * rayleigh + keep * move * (cur_bent + res_img) + move * move * res_bent
        return keep, move, lowest, following

    def step(p, carry):
        keep, move, before, rayleigh = [coef[i:i + 1] for i in range(4)]
        sum_start(p, sums_of(rayleigh))
        for t in range(count):
            first_stage(ops_left, t, top[t],
                        [(t, w) for w in range(terms)] + [(e[0], e[1]) for e in hop_rows[t]])
        sum_middle(p)
        for s in order:
            own[s] = second_stage(s, 0, own_columns[s])

        @pl.when(p == 0)
        def _():
            rim_end()

        halo_wait(p)
        for slot in range(4):
            halo_top[slot] = keep * halo_top[slot] + move * (halo_in[p, slot] - before * halo_top[slot])
            first_stage(ops_halo, slot, halo_top[slot], [(e[0], e[1]) for e in halo_rows[slot]])
        for s in order:
            total = own[s]
            if own_columns[s] < terms + 4:
                total = total + second_stage(s, own_columns[s], terms + 4)
            out[s] = masked(s, total)
            halo_start(out, p + 1, s, p < ITERS)

        keep, move, _, following = solve(p == 1, rayleigh, sum_end(p))
        initial = p == 0
        keep = jnp.where(initial, 0.0, keep)
        move = jnp.where(initial, 1.0, move)
        following = jnp.where(initial, 0.0, following)
        for s in range(count):
            cur[s] = keep * cur[s] + move * (img[s] - rayleigh * cur[s])
            img[s] = keep * img[s] + move * (top[s] - rayleigh * img[s])
            top[s] = keep * top[s] + move * (out[s] - rayleigh * top[s])
        for i, value in enumerate((keep, move, rayleigh, following)):
            coef[i:i + 1] = value
        return carry

    nothing = jnp.zeros((1, size), f32)
    for i, value in enumerate((nothing, nothing + 1.0, nothing, nothing)):
        coef[i:i + 1] = value
    lax.fori_loop(0, steps, step, 0)
    rayleigh = coef[3:4]
    sum_start(steps, sums_of(rayleigh))
    sum_middle(steps)
    keep, move, lowest, _ = solve(False, rayleigh, sum_end(steps))
    energy[...] = lowest[:, 0:1]
    for s in range(count):
        ritz[s] = keep * cur[s] + move * (img[s] - rayleigh * cur[s])


def on_device(left_env, right_env, hop_ops, start, left_dims, right_dims):
    count, terms, size = left_env.shape[0], left_env.shape[1], left_env.shape[2]
    n = lax.axis_size("sec")
    blocks = terms + 4
    steps = ITERS + 1
    inner = max(d for d in range(1, n + 1) if n % d == 0 and d * d <= n)
    dma = pltpu.SemaphoreType.DMA
    anywhere = pl.BlockSpec(memory_space=pl.ANY)
    scalars = pl.BlockSpec(memory_space=pltpu.SMEM)
    inside = pl.BlockSpec(memory_space=pltpu.VMEM)
    ritz, energy = pl.pallas_call(
        functools.partial(kernel, n, count, terms),
        out_shape=(jax.ShapeDtypeStruct((count, size, size), f32), jax.ShapeDtypeStruct((1, 1), f32)),
        in_specs=[anywhere] * 4 + [scalars] * 2,
        out_specs=(inside, inside),
        scratch_shapes=[
            pltpu.VMEM((count, terms, size, size), f32),
            pltpu.VMEM((count, terms, size, size), f32),
            pltpu.VMEM((count, 4, size, size), f32),
            pltpu.VMEM((2, 4, size, size), f32),
            pltpu.VMEM((count, blocks * size, 2 * size), bf16),
            pltpu.VMEM((count, blocks * size, 2 * size), bf16),
            pltpu.VMEM((4, 2 * size, 2 * size), bf16),
            pltpu.VMEM((count, 2 * size, blocks * size), bf16),
            pltpu.VMEM((count, size, size), f32),
            pltpu.VMEM((count, size, size), f32),
            pltpu.VMEM((count, size, size), f32),
            pltpu.VMEM((count, size, size), f32),
            pltpu.VMEM((count, size, size), f32),
            pltpu.VMEM((steps, 4, size, size), f32),
            pltpu.VMEM((4, size, size), f32),
            pltpu.VMEM((steps + 1, inner, 1, size), f32),
            pltpu.VMEM((steps + 1, n // inner, 1, size), f32),
            pltpu.VMEM((8, size), f32),
            dma((2 + 2 * count,)),
            dma((2,)), dma((2,)),
            dma((steps, 4)), dma((steps, 4)),
            dma((2, steps + 1)), dma((2, steps + 1)),
        ],
        compiler_params=pltpu.CompilerParams(
            collective_id=0, has_side_effects=True, vmem_limit_bytes=60 * 1024 * 1024),
    )(left_env, right_env, hop_ops, start, left_dims, right_dims)
    total_entries = count * n * size * size
    return ritz * jnp.sqrt(jnp.float32(total_entries)), jnp.reshape(energy, (1,))


def solution(mesh):
    in_specs = (
        P(("parts", "sec"), None, None, None),
        P(("parts", "sec"), None, None, None),
        P(("parts", "sec"), None, None, None),
        P(("parts", "sec"), None, None),
        P(("parts", "sec")),
        P(("parts", "sec")),
    )
    out_specs = (P(("parts", "sec"), None, None), P("parts"))
    return jax.shard_map(
        on_device, mesh=mesh, in_specs=in_specs, out_specs=out_specs, check_vma=False
    )
```

```python
import functools
import math

import jax
import jax.numpy as jnp
from jax import lax
from jax.experimental import pallas as pl
from jax.experimental.pallas import tpu as pltpu
from jax.sharding import PartitionSpec as P

ITERS = 4
EPSILON = 1e-12
MESH = pl.DeviceIdType.MESH
f32 = jnp.float32
bf16 = jnp.bfloat16


def halves(x):
    hi = x.astype(bf16)
    return hi, (x - hi.astype(f32)).astype(bf16)


def kernel(
    n, count, terms,
    left_env, right_env, hop_ops, start, left_dims, right_dims,
    ritz, energy,
    left_in, right_in, hop_in, rim, ops_left, ops_right, ops_halo, middle,
    cur, img, top, own, out, halo_in, halo_top, sums, coef,
    load_sem, rim_send, rim_recv, halo_send, halo_recv, sum_send, sum_recv,
):
    size = start.shape[1]
    me = lax.axis_index("sec")
    has_left, has_right = me > 0, me < n - 1
    left, right = lax.max(me - 1, 0), lax.min(me + 1, n - 1)
    steps = ITERS + 1
    peers = [lax.rem(me + j, n) for j in range(1, n)]

    loads = [pltpu.make_async_copy(start, top, load_sem.at[0]),
             pltpu.make_async_copy(hop_ops, hop_in, load_sem.at[1])]
    for s in range(count):
        loads.append(pltpu.make_async_copy(left_env.at[s], left_in.at[s], load_sem.at[2 + s]))
    for s in range(count):
        loads.append(pltpu.make_async_copy(right_env.at[s], right_in.at[s], load_sem.at[2 + count + s]))
    for load in loads:
        load.start()

    barrier = pltpu.get_barrier_semaphore()
    for device in peers:
        pl.semaphore_signal(barrier, inc=1, device_id={"sec": device}, device_id_type=MESH)

    rows = lax.broadcasted_iota(jnp.int32, (size, size), 0)
    cols = lax.broadcasted_iota(jnp.int32, (size, size), 1)
    lane = lax.broadcasted_iota(jnp.int32, (1, size), 1)

    def masked(s, x):
        return jnp.where((rows < left_dims[s]) & (cols < right_dims[s]), x, 0.0)

    halo_top[...] = jnp.zeros_like(halo_top)
    cur[...] = jnp.zeros_like(cur)
    img[...] = jnp.zeros_like(img)

    @pl.when(jnp.logical_not(has_left))
    def _():
        rim[...] = jnp.zeros_like(rim)
        for p in range(steps):
            halo_in[p, 0:2] = jnp.zeros((2, size, size), f32)

    @pl.when(jnp.logical_not(has_right))
    def _():
        for p in range(steps):
            halo_in[p, 2:4] = jnp.zeros((2, size, size), f32)

    scale = 1.0 / (6.0 * math.sqrt(count * n * size * size))
    loads[0].wait()
    for s in range(count):
        top[s] = masked(s, top[s]) * scale

    def halo_copy(src, p, s, slot):
        device = right if slot < 2 else left
        return pltpu.make_async_remote_copy(
            src_ref=src.at[s], dst_ref=halo_in.at[p, slot],
            send_sem=halo_send.at[p, slot], recv_sem=halo_recv.at[p, slot],
            device_id={"sec": device}, device_id_type=MESH)

    targets = {}
    for i in range(2):
        targets.setdefault(count - 2 + i, []).append(i)
        targets.setdefault(i, []).append(2 + i)

    def halo_start(src, p, s, more=True):
        for slot in targets.get(s, ()):
            @pl.when((has_right if slot < 2 else has_left) & more)
            def _():
                halo_copy(src, p, s, slot).start()

    def halo_wait(p):
        for s in targets:
            for slot in targets[s]:
                @pl.when(has_right if slot < 2 else has_left)
                def _():
                    halo_copy(out, p, s, slot).wait_send()

                @pl.when(has_left if slot < 2 else has_right)
                def _():
                    halo_copy(out, p, s, slot).wait_recv()

    def sum_start(p, values):
        line = jnp.zeros((1, size), f32)
        for i, value in enumerate(values):
            line = jnp.where(lane == i, jnp.sum(value, axis=(0, 1), keepdims=True), line)
        sums[p, me] = line
        for device in peers:
            pltpu.make_async_remote_copy(
                src_ref=sums.at[p, me], dst_ref=sums.at[p, me],
                send_sem=sum_send.at[p], recv_sem=sum_recv.at[p],
                device_id={"sec": device}, device_id_type=MESH).start()

    def sum_end(p):
        if n > 1:
            whole = sums.at[p, 0:n - 1]
            pltpu.make_async_copy(whole, whole, sum_recv.at[p]).wait()
            pltpu.make_async_copy(whole, whole, sum_send.at[p]).wait()
        line = jnp.sum(sums[p], axis=0)
        return [jnp.broadcast_to(jnp.sum(jnp.where(lane == i, line, 0.0), axis=1, keepdims=True), (1, size))
                for i in range(4)]

    def put(ref, index, row, x):
        hi, lo = halves(x)
        ref[index, row * size:(row + 1) * size, 0:size] = hi
        ref[index, row * size:(row + 1) * size, size:2 * size] = lo

    hop_rows = [[] for _ in range(count)]
    halo_rows = [[] for _ in range(4)]
    seconds = [[] for _ in range(count)]
    own_columns = []
    for s in range(count):
        column = terms
        for inside in (True, False):
            for k in (1, 2):
                for t, owner, flip in ((s + k, s, False), (s - k, s - k, True)):
                    if (0 <= t < count) != inside:
                        continue
                    entry = (s, column, owner, k, flip)
                    if inside:
                        hop_rows[t].append(entry)
                    else:
                        halo_rows[2 + t if t < 0 else 2 + t - count].append(entry)
                    seconds[s].append(entry)
                    column += 1
            if inside:
                own_columns.append(column)

    def hop(owner, index, flip):
        block = hop_in[owner, index] if owner >= 0 else rim[2 + owner, index]
        return block.T if flip else block

    loads[1].wait()
    for s in range(count):
        loads[2 + s].wait()
        for w in range(terms):
            put(ops_left, s, w, left_in[s, w])
        for i, (_, _, owner, k, flip) in enumerate(hop_rows[s]):
            put(ops_left, s, terms + i, hop(owner, 2 * k - 2, flip))
    pl.semaphore_wait(barrier, n - 1)
    for s in range(count):
        halo_start(top, 0, s)
    rim_copies = [
        pltpu.make_async_remote_copy(
            src_ref=src, dst_ref=dst, send_sem=rim_send.at[i], recv_sem=rim_recv.at[i],
            device_id={"sec": right}, device_id_type=MESH)
        for i, (src, dst) in enumerate((
            (hop_ops.at[count - 1], rim.at[1]),
            (hop_ops.at[count - 2, 2:4], rim.at[0, 2:4])))]

    @pl.when(has_right)
    def _():
        for copy in rim_copies:
            copy.start()

    for s in range(count):
        loads[2 + count + s].wait()
        for w in range(terms):
            put(ops_right, s, w, right_in[s, w])
        for _, column, owner, k, flip in seconds[s]:
            if owner >= 0:
                put(ops_right, s, column, hop(owner, 2 * k - 1, flip))
    for slot in range(4):
        for i, (_, _, owner, k, flip) in enumerate(halo_rows[slot]):
            if owner >= 0:
                put(ops_halo, slot, i, hop(owner, 2 * k - 2, flip))

    def rim_end():
        @pl.when(has_left)
        def _():
            for copy in rim_copies:
                copy.wait_recv()

        @pl.when(has_right)
        def _():
            for copy in rim_copies:
                copy.wait_send()

        for slot in range(4):
            for i, (_, _, owner, k, flip) in enumerate(halo_rows[slot]):
                if owner < 0:
                    put(ops_halo, slot, i, hop(owner, 2 * k - 2, flip))
        for s in range(count):
            for _, column, owner, k, flip in seconds[s]:
                if owner < 0:
                    put(ops_right, s, column, hop(owner, 2 * k - 1, flip))

    def first_stage(ops, index, x, targets_of):
        hi, lo = halves(x)
        line = jnp.concatenate([hi, lo], axis=1)
        both = jnp.concatenate([line, line], axis=0)
        chunk = 4
        for base in range(0, len(targets_of), chunk):
            some = targets_of[base:base + chunk]
            product = jnp.dot(ops[index, base * size:(base + len(some)) * size, :], both,
                              preferred_element_type=f32)
            for i, (s, column) in enumerate(some):
                y = product[i * size:(i + 1) * size]
                hi, lo = halves(y[:, :size] + y[:, size:])
                middle[s, 0:size, column * size:(column + 1) * size] = hi
                middle[s, size:2 * size, column * size:(column + 1) * size] = lo

    def second_stage(s, begin, end):
        product = jnp.dot(middle[s, :, begin * size:end * size], ops_right[s, begin * size:end * size, :],
                          preferred_element_type=f32)
        product = product[:size] + product[size:]
        return product[:, :size] + product[:, size:]

    order = []
    for s in range((count + 1) // 2):
        order += [s] if s == count - 1 - s else [s, count - 1 - s]

    def sums_of(rayleigh):
        values = [jnp.zeros((size, size), f32) for _ in range(4)]
        for s in range(count):
            residual = img[s] - rayleigh * cur[s]
            bent = top[s] - rayleigh * img[s]
            values[0] += residual * residual
            values[1] += residual * bent
            values[2] += cur[s] * bent
            values[3] += residual * img[s]
        return values

    def solve(first, rayleigh, values):
        res_sum, res_bent, cur_bent, res_img = values
        res_sq = res_sum + EPSILON
        res_norm = jnp.sqrt(res_sq)
        curvature = res_bent / res_sq
        lowest = (rayleigh + curvature) / 2 - jnp.sqrt(((rayleigh - curvature) / 2) ** 2 + res_norm * res_norm)
        slope = lowest - rayleigh
        length = jnp.sqrt(res_norm * res_norm + slope * slope)
        keep = jnp.where(first, 0.0, res_norm / length)
        move = jnp.where(first, lax.rsqrt(res_sum), slope / length / res_norm)
        following = keep * keep * rayleigh + keep * move * (cur_bent + res_img) + move * move * res_bent
        return keep, move, lowest, following

    def step(p, carry):
        keep, move, before, rayleigh = [coef[i:i + 1] for i in range(4)]
        sum_start(p, sums_of(rayleigh))
        for t in range(count):
            first_stage(ops_left, t, top[t],
                        [(t, w) for w in range(terms)] + [(e[0], e[1]) for e in hop_rows[t]])
        for s in order:
            own[s] = second_stage(s, 0, own_columns[s])

        @pl.when(p == 0)
        def _():
            rim_end()

        halo_wait(p)
        for slot in range(4):
            halo_top[slot] = keep * halo_top[slot] + move * (halo_in[p, slot] - before * halo_top[slot])
            first_stage(ops_halo, slot, halo_top[slot], [(e[0], e[1]) for e in halo_rows[slot]])
        for s in order:
            total = own[s]
            if own_columns[s] < terms + 4:
                total = total + second_stage(s, own_columns[s], terms + 4)
            out[s] = masked(s, total)
            halo_start(out, p + 1, s, p < ITERS)

        keep, move, _, following = solve(p == 1, rayleigh, sum_end(p))
        initial = p == 0
        keep = jnp.where(initial, 0.0, keep)
        move = jnp.where(initial, 1.0, move)
        following = jnp.where(initial, 0.0, following)
        for s in range(count):
            cur[s] = keep * cur[s] + move * (img[s] - rayleigh * cur[s])
            img[s] = keep * img[s] + move * (top[s] - rayleigh * img[s])
            top[s] = keep * top[s] + move * (out[s] - rayleigh * top[s])
        for i, value in enumerate((keep, move, rayleigh, following)):
            coef[i:i + 1] = value
        return carry

    nothing = jnp.zeros((1, size), f32)
    for i, value in enumerate((nothing, nothing + 1.0, nothing, nothing)):
        coef[i:i + 1] = value
    lax.fori_loop(0, steps, step, 0)
    rayleigh = coef[3:4]
    sum_start(steps, sums_of(rayleigh))
    keep, move, lowest, _ = solve(False, rayleigh, sum_end(steps))
    energy[...] = lowest[:, 0:1]
    for s in range(count):
        ritz[s] = keep * cur[s] + move * (img[s] - rayleigh * cur[s])


def on_device(left_env, right_env, hop_ops, start, left_dims, right_dims):
    count, terms, size = left_env.shape[0], left_env.shape[1], left_env.shape[2]
    n = lax.axis_size("sec")
    blocks = terms + 4
    steps = ITERS + 1
    dma = pltpu.SemaphoreType.DMA
    anywhere = pl.BlockSpec(memory_space=pl.ANY)
    scalars = pl.BlockSpec(memory_space=pltpu.SMEM)
    inside = pl.BlockSpec(memory_space=pltpu.VMEM)
    ritz, energy = pl.pallas_call(
        functools.partial(kernel, n, count, terms),
        out_shape=(jax.ShapeDtypeStruct((count, size, size), f32), jax.ShapeDtypeStruct((1, 1), f32)),
        in_specs=[anywhere] * 4 + [scalars] * 2,
        out_specs=(inside, inside),
        scratch_shapes=[
            pltpu.VMEM((count, terms, size, size), f32),
            pltpu.VMEM((count, terms, size, size), f32),
            pltpu.VMEM((count, 4, size, size), f32),
            pltpu.VMEM((2, 4, size, size), f32),
            pltpu.VMEM((count, blocks * size, 2 * size), bf16),
            pltpu.VMEM((count, blocks * size, 2 * size), bf16),
            pltpu.VMEM((4, 2 * size, 2 * size), bf16),
            pltpu.VMEM((count, 2 * size, blocks * size), bf16),
            pltpu.VMEM((count, size, size), f32),
            pltpu.VMEM((count, size, size), f32),
            pltpu.VMEM((count, size, size), f32),
            pltpu.VMEM((count, size, size), f32),
            pltpu.VMEM((count, size, size), f32),
            pltpu.VMEM((steps, 4, size, size), f32),
            pltpu.VMEM((4, size, size), f32),
            pltpu.VMEM((steps + 1, n, 1, size), f32),
            pltpu.VMEM((8, size), f32),
            dma((2 + 2 * count,)),
            dma((2,)), dma((2,)),
            dma((steps, 4)), dma((steps, 4)),
            dma((steps + 1,)), dma((steps + 1,)),
        ],
        compiler_params=pltpu.CompilerParams(
            collective_id=0, has_side_effects=True, vmem_limit_bytes=60 * 1024 * 1024),
    )(left_env, right_env, hop_ops, start, left_dims, right_dims)
    total_entries = count * n * size * size
    return ritz * jnp.sqrt(jnp.float32(total_entries)), jnp.reshape(energy, (1,))


def solution(mesh):
    in_specs = (
        P(("parts", "sec"), None, None, None),
        P(("parts", "sec"), None, None, None),
        P(("parts", "sec"), None, None, None),
        P(("parts", "sec"), None, None),
        P(("parts", "sec")),
        P(("parts", "sec")),
    )
    out_specs = (P(("parts", "sec"), None, None), P("parts"))
    return jax.shard_map(
        on_device, mesh=mesh, in_specs=in_specs, out_specs=out_specs, check_vma=False
    )
```

```python
import functools
import math

import jax
import jax.numpy as jnp
from jax import lax
from jax.experimental import pallas as pl
from jax.experimental.pallas import tpu as pltpu
from jax.sharding import PartitionSpec as P

ITERS = 4
EPSILON = 1e-12
MESH = pl.DeviceIdType.MESH
f32 = jnp.float32
bf16 = jnp.bfloat16


def halves(x):
    hi = x.astype(bf16)
    return hi, (x - hi.astype(f32)).astype(bf16)


def kernel(
    n, count, terms,
    left_env, right_env, hop_ops, start, left_dims, right_dims,
    ritz, energy,
    left_in, right_in, hop_in, rim, ops_left, ops_right, ops_halo, middle,
    cur, img, top, own, out, halo_in, halo_top, sums, coef,
    load_sem, rim_send, rim_recv, halo_send, halo_recv, sum_send, sum_recv,
):
    size = start.shape[1]
    me = lax.axis_index("sec")
    has_left, has_right = me > 0, me < n - 1
    left, right = lax.max(me - 1, 0), lax.min(me + 1, n - 1)
    steps = ITERS + 1
    peers = [lax.rem(me + j, n) for j in range(1, n)]

    barrier = pltpu.get_barrier_semaphore()
    for device in peers:
        pl.semaphore_signal(barrier, inc=1, device_id={"sec": device}, device_id_type=MESH)

    loads = [pltpu.make_async_copy(start, top, load_sem.at[0]),
             pltpu.make_async_copy(hop_ops, hop_in, load_sem.at[1])]
    for s in range(count):
        loads.append(pltpu.make_async_copy(left_env.at[s], left_in.at[s], load_sem.at[2 + s]))
    for s in range(count):
        loads.append(pltpu.make_async_copy(right_env.at[s], right_in.at[s], load_sem.at[2 + count + s]))
    for load in loads:
        load.start()

    rows = lax.broadcasted_iota(jnp.int32, (size, size), 0)
    cols = lax.broadcasted_iota(jnp.int32, (size, size), 1)
    lane = lax.broadcasted_iota(jnp.int32, (1, size), 1)

    def masked(s, x):
        return jnp.where((rows < left_dims[s]) & (cols < right_dims[s]), x, 0.0)

    halo_top[...] = jnp.zeros_like(halo_top)
    cur[...] = jnp.zeros_like(cur)
    img[...] = jnp.zeros_like(img)
    sums[0] = jnp.zeros((n, 1, size), f32)

    @pl.when(jnp.logical_not(has_left))
    def _():
        rim[...] = jnp.zeros_like(rim)
        for p in range(steps):
            halo_in[p, 0:2] = jnp.zeros((2, size, size), f32)

    @pl.when(jnp.logical_not(has_right))
    def _():
        for p in range(steps):
            halo_in[p, 2:4] = jnp.zeros((2, size, size), f32)

    scale = 1.0 / (6.0 * math.sqrt(count * n * size * size))
    loads[0].wait()
    for s in range(count):
        top[s] = masked(s, top[s]) * scale

    def halo_copy(src, p, s, slot):
        device = right if slot < 2 else left
        return pltpu.make_async_remote_copy(
            src_ref=src.at[s], dst_ref=halo_in.at[p, slot],
            send_sem=halo_send.at[p, slot], recv_sem=halo_recv.at[p, slot],
            device_id={"sec": device}, device_id_type=MESH)

    targets = {}
    for i in range(2):
        targets.setdefault(count - 2 + i, []).append(i)
        targets.setdefault(i, []).append(2 + i)

    def halo_start(src, p, s, more=True):
        for slot in targets.get(s, ()):
            @pl.when((has_right if slot < 2 else has_left) & more)
            def _():
                halo_copy(src, p, s, slot).start()

    def halo_wait(p):
        for s in targets:
            for slot in targets[s]:
                @pl.when(has_right if slot < 2 else has_left)
                def _():
                    halo_copy(out, p, s, slot).wait_send()

                @pl.when(has_left if slot < 2 else has_right)
                def _():
                    halo_copy(out, p, s, slot).wait_recv()

    def sum_start(p, values):
        line = jnp.zeros((1, size), f32)
        for i, value in enumerate(values):
            line = jnp.where(lane == i, jnp.sum(value, axis=(0, 1), keepdims=True), line)
        sums[p, me] = line
        for device in peers:
            pltpu.make_async_remote_copy(
                src_ref=sums.at[p, me], dst_ref=sums.at[p, me],
                send_sem=sum_send.at[p], recv_sem=sum_recv.at[p],
                device_id={"sec": device}, device_id_type=MESH).start()

    def sum_end(p):
        if n > 1:
            @pl.when(p > 0)
            def _():
                whole = sums.at[p, 0:n - 1]
                pltpu.make_async_copy(whole, whole, sum_recv.at[p]).wait()
                pltpu.make_async_copy(whole, whole, sum_send.at[p]).wait()

        line = jnp.sum(sums[p], axis=0)
        return [jnp.broadcast_to(jnp.sum(jnp.where(lane == i, line, 0.0), axis=1, keepdims=True), (1, size))
                for i in range(4)]

    def put(ref, index, row, x):
        hi, lo = halves(x)
        ref[index, row * size:(row + 1) * size, 0:size] = hi
        ref[index, row * size:(row + 1) * size, size:2 * size] = lo

    hop_rows = [[] for _ in range(count)]
    halo_rows = [[] for _ in range(4)]
    seconds = [[] for _ in range(count)]
    own_columns = []
    for s in range(count):
        column = terms
        for inside in (True, False):
            for k in (1, 2):
                for t, owner, flip in ((s + k, s, False), (s - k, s - k, True)):
                    if (0 <= t < count) != inside:
                        continue
                    entry = (s, column, owner, k, flip)
                    if inside:
                        hop_rows[t].append(entry)
                    else:
                        halo_rows[2 + t if t < 0 else 2 + t - count].append(entry)
                    seconds[s].append(entry)
                    column += 1
            if inside:
                own_columns.append(column)

    def hop(owner, index, flip):
        block = hop_in[owner, index] if owner >= 0 else rim[2 + owner, index]
        return block.T if flip else block

    loads[1].wait()
    for s in range(count):
        loads[2 + s].wait()
        for w in range(terms):
            put(ops_left, s, w, left_in[s, w])
        for i, (_, _, owner, k, flip) in enumerate(hop_rows[s]):
            put(ops_left, s, terms + i, hop(owner, 2 * k - 2, flip))
    pl.semaphore_wait(barrier, n - 1)
    for s in range(count):
        halo_start(top, 0, s)
    rim_copies = [
        pltpu.make_async_remote_copy(
            src_ref=src, dst_ref=dst, send_sem=rim_send.at[i], recv_sem=rim_recv.at[i],
            device_id={"sec": right}, device_id_type=MESH)
        for i, (src, dst) in enumerate((
            (hop_ops.at[count - 1], rim.at[1]),
            (hop_ops.at[count - 2, 2:4], rim.at[0, 2:4])))]

    @pl.when(has_right)
    def _():
        for copy in rim_copies:
            copy.start()

    for s in range(count):
        loads[2 + count + s].wait()
        for w in range(terms):
            put(ops_right, s, w, right_in[s, w])
        for _, column, owner, k, flip in seconds[s]:
            if owner >= 0:
                put(ops_right, s, column, hop(owner, 2 * k - 1, flip))
    for slot in range(4):
        for i, (_, _, owner, k, flip) in enumerate(halo_rows[slot]):
            if owner >= 0:
                put(ops_halo, slot, i, hop(owner, 2 * k - 2, flip))

    def rim_end():
        @pl.when(has_left)
        def _():
            for copy in rim_copies:
                copy.wait_recv()

        @pl.when(has_right)
        def _():
            for copy in rim_copies:
                copy.wait_send()

        for slot in range(4):
            for i, (_, _, owner, k, flip) in enumerate(halo_rows[slot]):
                if owner < 0:
                    put(ops_halo, slot, i, hop(owner, 2 * k - 2, flip))
        for s in range(count):
            for _, column, owner, k, flip in seconds[s]:
                if owner < 0:
                    put(ops_right, s, column, hop(owner, 2 * k - 1, flip))

    def first_stage(ops, index, x, targets_of):
        hi, lo = halves(x)
        line = jnp.concatenate([hi, lo], axis=1)
        both = jnp.concatenate([line, line], axis=0)
        chunk = 4
        for base in range(0, len(targets_of), chunk):
            some = targets_of[base:base + chunk]
            product = jnp.dot(ops[index, base * size:(base + len(some)) * size, :], both,
                              preferred_element_type=f32)
            for i, (s, column) in enumerate(some):
                y = product[i * size:(i + 1) * size]
                hi, lo = halves(y[:, :size] + y[:, size:])
                middle[s, 0:size, column * size:(column + 1) * size] = hi
                middle[s, size:2 * size, column * size:(column + 1) * size] = lo

    def second_stage(s, begin, end):
        product = jnp.dot(middle[s, :, begin * size:end * size], ops_right[s, begin * size:end * size, :],
                          preferred_element_type=f32)
        product = product[:size] + product[size:]
        return product[:, :size] + product[:, size:]

    order = []
    for s in range((count + 1) // 2):
        order += [s] if s == count - 1 - s else [s, count - 1 - s]

    def sums_of(rayleigh):
        values = [jnp.zeros((size, size), f32) for _ in range(4)]
        for s in range(count):
            residual = img[s] - rayleigh * cur[s]
            bent = top[s] - rayleigh * img[s]
            values[0] += residual * residual
            values[1] += residual * bent
            values[2] += cur[s] * bent
            values[3] += residual * img[s]
        return values

    def solve(first, rayleigh, values):
        res_sum, res_bent, cur_bent, res_img = values
        res_sq = res_sum + EPSILON
        res_norm = jnp.sqrt(res_sq)
        curvature = res_bent / res_sq
        lowest = (rayleigh + curvature) / 2 - jnp.sqrt(((rayleigh - curvature) / 2) ** 2 + res_norm * res_norm)
        slope = lowest - rayleigh
        length = jnp.sqrt(res_norm * res_norm + slope * slope)
        keep = jnp.where(first, 0.0, res_norm / length)
        move = jnp.where(first, lax.rsqrt(res_sum), slope / length / res_norm)
        following = keep * keep * rayleigh + keep * move * (cur_bent + res_img) + move * move * res_bent
        return keep, move, lowest, following

    def step(p, carry):
        keep, move, before, rayleigh = [coef[i:i + 1] for i in range(4)]
        @pl.when(p > 0)
        def _():
            sum_start(p, sums_of(rayleigh))

        for t in range(count):
            first_stage(ops_left, t, top[t],
                        [(t, w) for w in range(terms)] + [(e[0], e[1]) for e in hop_rows[t]])
        for s in order:
            own[s] = second_stage(s, 0, own_columns[s])

        @pl.when(p == 0)
        def _():
            rim_end()

        halo_wait(p)
        for slot in range(4):
            halo_top[slot] = keep * halo_top[slot] + move * (halo_in[p, slot] - before * halo_top[slot])
            first_stage(ops_halo, slot, halo_top[slot], [(e[0], e[1]) for e in halo_rows[slot]])
        for s in order:
            total = own[s]
            if own_columns[s] < terms + 4:
                total = total + second_stage(s, own_columns[s], terms + 4)
            out[s] = masked(s, total)
            halo_start(out, p + 1, s, p < ITERS)

        keep, move, _, following = solve(p == 1, rayleigh, sum_end(p))
        initial = p == 0
        keep = jnp.where(initial, 0.0, keep)
        move = jnp.where(initial, 1.0, move)
        following = jnp.where(initial, 0.0, following)
        for s in range(count):
            cur[s] = keep * cur[s] + move * (img[s] - rayleigh * cur[s])
            img[s] = keep * img[s] + move * (top[s] - rayleigh * img[s])
            top[s] = keep * top[s] + move * (out[s] - rayleigh * top[s])
        for i, value in enumerate((keep, move, rayleigh, following)):
            coef[i:i + 1] = value
        return carry

    nothing = jnp.zeros((1, size), f32)
    for i, value in enumerate((nothing, nothing + 1.0, nothing, nothing)):
        coef[i:i + 1] = value
    lax.fori_loop(0, steps, step, 0)
    rayleigh = coef[3:4]
    sum_start(steps, sums_of(rayleigh))
    keep, move, lowest, _ = solve(False, rayleigh, sum_end(steps))
    energy[...] = lowest[:, 0:1]
    for s in range(count):
        ritz[s] = keep * cur[s] + move * (img[s] - rayleigh * cur[s])


def on_device(left_env, right_env, hop_ops, start, left_dims, right_dims):
    count, terms, size = left_env.shape[0], left_env.shape[1], left_env.shape[2]
    n = lax.axis_size("sec")
    blocks = terms + 4
    steps = ITERS + 1
    dma = pltpu.SemaphoreType.DMA
    anywhere = pl.BlockSpec(memory_space=pl.ANY)
    scalars = pl.BlockSpec(memory_space=pltpu.SMEM)
    inside = pl.BlockSpec(memory_space=pltpu.VMEM)
    ritz, energy = pl.pallas_call(
        functools.partial(kernel, n, count, terms),
        out_shape=(jax.ShapeDtypeStruct((count, size, size), f32), jax.ShapeDtypeStruct((1, 1), f32)),
        in_specs=[anywhere] * 4 + [scalars] * 2,
        out_specs=(inside, inside),
        scratch_shapes=[
            pltpu.VMEM((count, terms, size, size), f32),
            pltpu.VMEM((count, terms, size, size), f32),
            pltpu.VMEM((count, 4, size, size), f32),
            pltpu.VMEM((2, 4, size, size), f32),
            pltpu.VMEM((count, blocks * size, 2 * size), bf16),
            pltpu.VMEM((count, blocks * size, 2 * size), bf16),
            pltpu.VMEM((4, 2 * size, 2 * size), bf16),
            pltpu.VMEM((count, 2 * size, blocks * size), bf16),
            pltpu.VMEM((count, size, size), f32),
            pltpu.VMEM((count, size, size), f32),
            pltpu.VMEM((count, size, size), f32),
            pltpu.VMEM((count, size, size), f32),
            pltpu.VMEM((count, size, size), f32),
            pltpu.VMEM((steps, 4, size, size), f32),
            pltpu.VMEM((4, size, size), f32),
            pltpu.VMEM((steps + 1, n, 1, size), f32),
            pltpu.VMEM((8, size), f32),
            dma((2 + 2 * count,)),
            dma((2,)), dma((2,)),
            dma((steps, 4)), dma((steps, 4)),
            dma((steps + 1,)), dma((steps + 1,)),
        ],
        compiler_params=pltpu.CompilerParams(
            collective_id=0, has_side_effects=True, vmem_limit_bytes=60 * 1024 * 1024),
    )(left_env, right_env, hop_ops, start, left_dims, right_dims)
    total_entries = count * n * size * size
    return ritz * jnp.sqrt(jnp.float32(total_entries)), jnp.reshape(energy, (1,))


def solution(mesh):
    in_specs = (
        P(("parts", "sec"), None, None, None),
        P(("parts", "sec"), None, None, None),
        P(("parts", "sec"), None, None, None),
        P(("parts", "sec"), None, None),
        P(("parts", "sec")),
        P(("parts", "sec")),
    )
    out_specs = (P(("parts", "sec"), None, None), P("parts"))
    return jax.shard_map(
        on_device, mesh=mesh, in_specs=in_specs, out_specs=out_specs, check_vma=False
    )
```
